32 devices in a mesh: heads: 4 (over y, x), ctx: 8 (over z, core).
Axes of the slice: x: 2, y: 2, z: 4, core: 2. Of those that a mesh axis runs over, the one named last changes fastest.
Arguments:
- query_vectors: bfloat16 [1024, 4, 640], P('ctx', 'heads'), may hold values from -6 to 6
- key_vectors: bfloat16 [1024, 4, 128], P('ctx', 'heads'), may hold values from -6 to 6
- value_vectors: bfloat16 [1024, 4, 128], P('ctx', 'heads'), may hold values from -6 to 6
- log_gate: float32 [4, 1024], P('heads', 'ctx'), may hold values from -1 to 0, as said below
- doc_start: int32 [8], P('ctx'), may hold values from 1 to 128
- norm_gain: float32 [4, 640], P('heads'), may hold values from 0.1 to 1.9
- out_weight: bfloat16 [2560, 5120], P('heads'), may hold values from -0.125 to 0.125
Outputs:
- mixed_out: bfloat16 [1024, 5120], P('ctx', 'heads')
- prefix_state: bfloat16 [4, 8, 8256, 128], P('heads', 'ctx')
The draws below stay inside these ranges and needn't reach their ends.
Inputs may be any that keep to these rules, and one draw needn't show every extreme that they name: log_gate is never positive.
All inputs are finite; a program needn't handle non-finite values.
Results may differ from the reference program's by a relative error of at most 0.014.
Values may be sent and summed in bfloat16 or wider, within the bound.
A program may use at most 192 MiB of HBM per device.

```python
import math
import jax
import jax.numpy as jnp
import numpy as np
from jax import lax

D = 5120
DH = 128
GROUP = 5
TOK_DEV = 128
COMMON_KV_GROUPS = 4
TOKENS = 1024
FEAT = 8256
N_CTX = 8


def draw_log_gate(key, part):
    entropy_seed_array = jax.random.split(jax.random.fold_in(key, 11), 5)
    shards = TOKENS // TOK_DEV
    fast_share = 0.5
    fast_heads = jax.random.uniform(entropy_seed_array[0], (COMMON_KV_GROUPS, 1)) < fast_share
    token_factor = jax.random.uniform(entropy_seed_array[1], (COMMON_KV_GROUPS, TOKENS), minval=0.5, maxval=1.5)
    shard_factor = jax.random.uniform(entropy_seed_array[2], (COMMON_KV_GROUPS, shards), minval=0.5, maxval=1.5)
    shard_factor = jnp.repeat(shard_factor, TOK_DEV, axis=1)
    decay_rate = jnp.where(fast_heads, 1.0 / 40.0, 0.4 / TOKENS) * token_factor * shard_factor
    destination_indices = jax.random.randint(entropy_seed_array[3], (COMMON_KV_GROUPS, 2, 1), 0, TOKENS)
    packet_extent_count = jnp.log(jax.random.uniform(entropy_seed_array[4], (COMMON_KV_GROUPS, 2, 1), minval=0.5, maxval=0.8))
    sequence_index = jnp.arange(TOKENS)[None, None, :]
    packet_tally = jnp.sum(jnp.where(sequence_index == destination_indices, packet_extent_count, 0.0), axis=1)
    return (packet_tally - decay_rate).astype(jnp.float32)


def draw_doc_start(key, part):
    entropy_seed_array = jax.random.split(jax.random.fold_in(key, 23), 3)
    shards = TOKENS // TOK_DEV
    pick_draw = jax.random.randint(entropy_seed_array[0], (shards,), 0, 32)
    place_draw = jax.random.randint(entropy_seed_array[1], (shards,), 1, TOK_DEV)
    forced_shard = jax.random.randint(entropy_seed_array[2], (), 1, shards)
    shard_index = jnp.arange(shards)
    first_shard = shard_index == 0
    chosen = ((pick_draw == 0) | (shard_index == forced_shard)) & jnp.logical_not(first_shard)
    return jnp.where(chosen, place_draw, TOK_DEV).astype(jnp.int32)


def block_levels(stream_key, extent, cuts, least, high):
    level, own = 1.0, jax.random.fold_in(stream_key, 6)
    for axis_at, parts in cuts:
        heights = jnp.exp(jax.random.uniform(jax.random.fold_in(own, axis_at), (parts,), jnp.float32, least / len(cuts), high / len(cuts)))
        level = level * jnp.repeat(heights, extent[axis_at] // parts).reshape([-1 if axis == axis_at else 1 for axis in range(len(extent))])
    return level


def centred(stream_key, extent, spread, limit, cuts=(), kind=jnp.bfloat16):
    loudness = block_levels(stream_key, extent, cuts, -0.22, 0.18) if cuts else 1.0
    array = jax.random.normal(stream_key, extent, jnp.float32) * spread * loudness
    return jnp.minimum(jnp.maximum(array, -limit), limit).astype(kind)


def setup_inputs(seed: int = 0) -> dict:
    seeds = jax.random.split(jax.random.key(seed), 8)
    return {
        "query_vectors": centred(seeds[0], (TOKENS, COMMON_KV_GROUPS, GROUP * DH), 1.0, 6.0, ((0, 8), (1, 4))),
        "key_vectors": centred(seeds[1], (TOKENS, COMMON_KV_GROUPS, DH), 1.0, 6.0, ((0, 8), (1, 4))),
        "value_vectors": centred(seeds[2], (TOKENS, COMMON_KV_GROUPS, DH), 1.0, 6.0, ((0, 8), (1, 4))),
        "log_gate": draw_log_gate(jax.random.fold_in(seeds[7], 71), 0),
        "doc_start": draw_doc_start(jax.random.fold_in(seeds[7], 71), 0),
        "norm_gain": jnp.clip(1.0 + 0.18 * jax.random.normal(seeds[5], (COMMON_KV_GROUPS, GROUP * DH), jnp.float32), 0.1, 1.9),
        "out_weight": centred(seeds[6], (COMMON_KV_GROUPS * GROUP * DH, D), (COMMON_KV_GROUPS * GROUP * DH) ** -0.5, 0.125, ((0, 4),)),
    }


ROOT_TWO = math.sqrt(2.0)

def expand(columns):
    rows_total = columns.shape[0]
    pieces = []
    for start_row in range(rows_total):
        scale_col = np.concatenate([np.ones((1, 1)), np.full((rows_total - start_row - 1, 1), ROOT_TWO)], axis=0)
        scale_col = jnp.asarray(scale_col, columns.dtype)
        pieces.append(columns[start_row:start_row + 1] * columns[start_row:] * scale_col)
    return jnp.concatenate(pieces, axis=0).astype(jnp.bfloat16)

def block_state(key_rows, value_rows, cumulative, boundary):
    block_len = key_rows.shape[0]
    sequence_index = jnp.arange(block_len, dtype=jnp.int32)
    doc_begin = jnp.where(boundary < block_len, boundary, 0)
    weights = jnp.where(sequence_index >= doc_begin, jnp.exp(cumulative[-1] - cumulative), 0.0)
    weighted = (value_rows.astype(jnp.float32) * weights[:, None]).astype(jnp.bfloat16)
    key_features = expand(key_rows.astype(jnp.float32).T)
    local_state = jnp.dot(key_features, weighted, preferred_element_type=jnp.float32)
    carry_factor = jnp.where(boundary >= block_len, jnp.exp(cumulative[-1]), 0.0)
    return (local_state, carry_factor)

def block_output(query_rows, key_rows, value_rows, cumulative, boundary, prefix_rows, gain_row):
    block_len, row_width = query_rows.shape
    head_size = key_rows.shape[1]
    groups = row_width // head_size
    grouped = query_rows.reshape(block_len, groups, head_size)
    products = jnp.einsum('tgd,sd->gts', grouped.astype(jnp.float32), key_rows.astype(jnp.float32))
    sequence_index = jnp.arange(block_len, dtype=jnp.int32)
    allowed = (sequence_index[None, :] <= sequence_index[:, None]) & jnp.logical_not((sequence_index[None, :] < boundary) & (sequence_index[:, None] >= boundary))
    decay_mask = jnp.where(allowed, jnp.exp(jnp.minimum(cumulative[:, None] - cumulative[None, :], 0.0)), 0.0)
    scores = (products * products * decay_mask[None]).astype(jnp.bfloat16)
    local_out = jnp.einsum('gts,sd->tgd', scores.astype(jnp.float32), value_rows.astype(jnp.float32))
    read_scale = jnp.where(sequence_index < boundary, jnp.exp(cumulative), 0.0)
    carried = []
    for group_index in range(groups):
        query_features = expand(grouped[:, group_index, :].astype(jnp.float32).T)
        carried.append(jnp.dot(query_features.T, prefix_rows, preferred_element_type=jnp.float32))
    carried = jnp.stack(carried, axis=1) * read_scale[:, None, None]
    summed = local_out + carried
    normed = summed * lax.rsqrt(lax.optimization_barrier(jnp.mean(summed * summed, axis=-1, keepdims=True)) + 1e-06)
    return (normed.reshape(block_len, row_width) * gain_row).astype(jnp.bfloat16)

def reference(query_vectors, key_vectors, value_vectors, log_gate, doc_start, norm_gain, out_weight):
    row_width = GROUP * DH
    partials = []
    states = []
    for head_index in range(COMMON_KV_GROUPS):
        query_blocks = query_vectors[:, head_index, :].reshape(N_CTX, TOK_DEV, row_width)
        key_blocks = key_vectors[:, head_index, :].reshape(N_CTX, TOK_DEV, DH)
        value_blocks = value_vectors[:, head_index, :].reshape(N_CTX, TOK_DEV, DH)
        gate_blocks = log_gate[head_index].reshape(N_CTX, TOK_DEV)
        gain_row = norm_gain[head_index]

        def advance_block(running, blocks):
            query_rows, key_rows, value_rows, gate_rows, boundary = blocks
            cumulative = jnp.cumsum(gate_rows)
            local_state, carry_factor = block_state(key_rows, value_rows, cumulative, boundary)
            prefix_rows = running.astype(jnp.bfloat16)
            retained = block_output(query_rows, key_rows, value_rows, cumulative, boundary, prefix_rows, gain_row)
            return (carry_factor * running + local_state, (retained, prefix_rows))
        start_state = jnp.zeros((FEAT, DH), jnp.float32)
        _, (retained_all, prefix_all) = lax.scan(advance_block, start_state, (query_blocks, key_blocks, value_blocks, gate_blocks, doc_start))
        rows_of_head = out_weight[head_index * row_width:(head_index + 1) * row_width]
        partial_value = jnp.dot(retained_all.reshape(TOKENS, row_width), rows_of_head, preferred_element_type=jnp.float32)
        partial_value = lax.optimization_barrier(partial_value.astype(jnp.bfloat16)).astype(jnp.float32)
        partials.append(partial_value)
        states.append(prefix_all)
    mixed_out = partials[0]
    for partial_value in partials[1:]:
        mixed_out = mixed_out + partial_value
    return (mixed_out.astype(jnp.bfloat16), jnp.stack(states, axis=0))
```

```python
import functools
import math

import jax
import jax.numpy as jnp
from jax import lax
from jax.experimental import pallas as pl
from jax.experimental.pallas import tpu as pltpu
from jax.sharding import PartitionSpec as P

ROOT_TWO = math.sqrt(2.0)
NT = (((1,), (1,)), ((), ()))
PER_STEP = 8
CHUNK = 8


def offset(i, size):
    return i * size - i * (i - 1) // 2


def attend_kernel(block, groups, q_ref, own_ref, all_ref, wt_ref, cum_ref, doc_ref, gain_ref, out_ref):
    size = q_ref.shape[1] // groups
    slots = all_ref.shape[0]
    f32 = jnp.float32
    queries = jnp.concatenate([q_ref[:, g * size : (g + 1) * size] for g in range(groups)], axis=0)
    boundary = doc_ref[0]
    cum_row = jnp.broadcast_to(cum_ref[...], (block, block))
    cum_col = cum_row.T
    at_t = lax.broadcasted_iota(jnp.int32, (block, block), 0)
    at_s = lax.broadcasted_iota(jnp.int32, (block, block), 1)
    allowed = (at_s <= at_t) & jnp.logical_not((at_s < boundary) & (at_t >= boundary))
    decay = jnp.where(allowed, jnp.exp(jnp.minimum(cum_col - cum_row, 0.0)), 0.0)
    read = jnp.where(at_t < boundary, jnp.exp(cum_col), 0.0)

    def part(keys, values, factor):
        products = lax.dot_general(queries, keys, NT, preferred_element_type=f32)
        scores = products * products * jnp.concatenate([factor] * groups, axis=0)
        return jnp.dot(scores.astype(jnp.bfloat16), values, preferred_element_type=f32)

    summed = part(own_ref[:, :size], own_ref[:, size:], decay)
    per = min(CHUNK, slots)
    for first in range(0, slots, per):
        keys = all_ref[first : first + per, :block, :size].reshape(per * block, size)
        values = all_ref[first : first + per, :block, size:].reshape(per * block, size)
        factor = jnp.concatenate(
            [read * wt_ref[:, (first + c) * block : (first + c + 1) * block] for c in range(per)], axis=1
        )
        summed = summed + part(keys, values, factor)
    normed = summed * lax.rsqrt(jnp.mean(summed * summed, axis=-1, keepdims=True) + 1e-6)
    for g in range(groups):
        lanes = slice(g * size, (g + 1) * size)
        rows = normed[g * block : (g + 1) * block]
        out_ref[:, lanes] = (rows * gain_ref[:, lanes]).astype(out_ref.dtype)


def state_kernel(block, all_ref, wt_ref, out_ref, keys_t, scaled, values, acc):
    slots = all_ref.shape[0]
    size = all_ref.shape[2] // 2
    per = min(CHUNK, slots)
    chunks = slots // per
    span = per * block

    def chunk(index):
        for c in range(per):
            lanes = slice(c * block, (c + 1) * block)
            turned = all_ref[index * per + c, :block, :size].astype(jnp.float32).T
            keys_t[:, lanes] = turned.astype(jnp.bfloat16)
            weight = wt_ref[:, pl.ds(pl.multiple_of((index * per + c) * block, block), block)]
            scaled[:, lanes] = turned * weight
            values[lanes, :] = all_ref[index * per + c, :block, size:]
        for a in range(size - 16, -1, -16):
            rows = size - a

            def step(s, carry):
                pieces = []
                firsts = []
                for u in range(PER_STEP):
                    i = a + 15 - (s * PER_STEP + u)
                    row = jnp.broadcast_to(scaled[pl.ds(i, 1), :], (16, span)).astype(jnp.bfloat16)
                    pieces.append(
                        (keys_t[a:, :].reshape(rows // 16, 16, span) * row[None]).reshape(rows, span)
                    )
                    firsts.append(i)
                product = jnp.dot(
                    jnp.concatenate(pieces, axis=0), values[...], preferred_element_type=jnp.float32
                )
                at = lax.broadcasted_iota(jnp.int32, (rows, size), 0) + a
                for u, i in enumerate(firsts):
                    piece = product[u * rows : (u + 1) * rows]
                    piece = jnp.where(at == i, piece, piece * ROOT_TWO)
                    place = pl.ds(offset(i, size) - (i - a), rows)
                    if chunks == 1:
                        acc[place, :] = piece
                    else:
                        acc[place, :] = acc[place, :] + jnp.where(at < i, 0.0, piece)
                return carry

            lax.fori_loop(0, 16 // PER_STEP, step, 0)

    if chunks == 1:
        chunk(0)
    else:
        acc[...] = jnp.zeros_like(acc)
        lax.fori_loop(0, chunks, lambda index, carry: (chunk(index), carry)[1], 0)
    out_ref[...] = acc[...].astype(out_ref.dtype)


def token_weights(gates, starts, me):
    slots, block = gates.shape
    token = jnp.arange(block, dtype=jnp.int32)
    cumulative = jnp.sum(
        jnp.where(token[None, :, None] >= token[None, None, :], gates[:, None, :], 0.0), axis=2
    )
    total = cumulative[:, -1]
    slot = jnp.arange(slots, dtype=jnp.int32)
    between = (slot[None, :] > slot[:, None]) & (slot[None, :] < me)
    later = jnp.sum(jnp.where(between, total[None, :], 0.0), axis=1)
    cut = jnp.any(between & (starts < block)[None, :], axis=1)
    begin = jnp.where(starts < block, starts, 0)
    live = (slot < me) & jnp.logical_not(cut)
    keep = live[:, None] & (token[None, :] >= begin[:, None])
    exponent = (total[:, None] - cumulative) + later[:, None]
    return jnp.where(keep, jnp.exp(exponent), 0.0)


def on_device(query_vectors, key_vectors, value_vectors, log_gate, doc_start, norm_gain, out_weight):
    bf16, f32 = jnp.bfloat16, jnp.float32
    block, _, size = key_vectors.shape
    groups = query_vectors.shape[2] // size
    features = size * (size + 1) // 2
    me = lax.axis_index("ctx")
    slots = lax.axis_size("ctx")

    gate = log_gate
    high = lax.reduce_precision(gate, 8, 7)
    middle = lax.reduce_precision(gate - high, 8, 7)
    low = gate - high - middle
    start = jnp.broadcast_to(doc_start.astype(f32)[:, None], (1, block))
    extra = jnp.concatenate(
        [jnp.concatenate([high, middle], axis=1), jnp.concatenate([low, start], axis=1)], axis=0
    ).astype(bf16)
    own = jnp.concatenate([key_vectors[:, 0, :], value_vectors[:, 0, :]], axis=1)
    sent = jnp.concatenate([own, jnp.pad(extra, ((0, 14), (0, 0)))], axis=0)
    gathered = lax.all_gather(sent, "ctx", axis=0, tiled=False)

    extras = gathered[:, block : block + 2, :].astype(f32)
    gates = extras[:, 0, :block] + extras[:, 0, block:] + extras[:, 1, :block]
    starts = extras[:, 1, block].astype(jnp.int32)
    weights = token_weights(gates, starts, me).reshape(1, slots * block)
    token = jnp.arange(block, dtype=jnp.int32)
    cumulative = jnp.sum(jnp.where(token[:, None] >= token[None, :], gate, 0.0), axis=1)[None]

    vmem = pl.BlockSpec(memory_space=pltpu.VMEM)
    retained = pl.pallas_call(
        functools.partial(attend_kernel, block, groups),
        out_shape=jax.ShapeDtypeStruct((block, groups * size), bf16),
        in_specs=[vmem] * 5 + [pl.BlockSpec(memory_space=pltpu.SMEM), vmem],
        out_specs=vmem,
        compiler_params=pltpu.CompilerParams(vmem_limit_bytes=48 * 2**20),
    )(query_vectors[:, 0, :], own, gathered, weights, cumulative, doc_start, norm_gain)
    partial = jnp.dot(retained, out_weight, preferred_element_type=f32).astype(bf16)
    mixed_out = lax.psum_scatter(partial, "heads", scatter_dimension=1, tiled=True)

    span = min(CHUNK, slots) * block
    prefix = pl.pallas_call(
        functools.partial(state_kernel, block),
        out_shape=jax.ShapeDtypeStruct((features, size), bf16),
        in_specs=[vmem] * 2,
        out_specs=vmem,
        scratch_shapes=[
            pltpu.VMEM((size, span), bf16),
            pltpu.VMEM((size, span), f32),
            pltpu.VMEM((span, size), bf16),
            pltpu.VMEM((features, size), f32),
        ],
        compiler_params=pltpu.CompilerParams(vmem_limit_bytes=48 * 2**20),
        cost_estimate=pl.CostEstimate(
            flops=2 * features * slots * block * size,
            bytes_accessed=2 * features * size + 4 * slots * block * size,
            transcendentals=0,
        ),
    )(gathered, weights)
    return (mixed_out, prefix[None, None])


def solution(mesh):
    placed = (
        P("ctx", "heads", None),
        P("ctx", "heads", None),
        P("ctx", "heads", None),
        P("heads", "ctx"),
        P("ctx"),
        P("heads", None),
        P("heads", None),
    )
    return jax.shard_map(
        on_device,
        mesh=mesh,
        in_specs=placed,
        out_specs=(P("ctx", "heads"), P("heads", "ctx", None, None)),
        check_vma=False,
    )
```

```python
import functools
import math

import jax
import jax.numpy as jnp
from jax import lax
from jax.experimental import pallas as pl
from jax.experimental.pallas import tpu as pltpu
from jax.sharding import PartitionSpec as P

ROOT_TWO = math.sqrt(2.0)
NT = (((1,), (1,)), ((), ()))
MESH = pl.DeviceIdType.MESH
PER_STEP = 8
CHUNK = 8
EXTRA = 16


def offset(i, size):
    return i * size - i * (i - 1) // 2


def running_sum(rows):
    lane = lax.broadcasted_iota(jnp.int32, rows.shape, 1)
    shift = 1
    while shift < rows.shape[1]:
        rows = rows + jnp.where(lane >= shift, pltpu.roll(rows, shift, axis=1), 0.0)
        shift *= 2
    return rows


def kernel(
    slots, heads, q_ref, k_ref, v_ref, gate_ref, doc_ref, gain_ref, weight_hbm,
    mixed_ref, prefix_ref,
    shared, token_weight, projection, retained, outgoing, incoming, keys_t, scaled, values, acc,
    load_sem, gather_send, gather_recv, part_send, part_recv,
):
    bf16, f32 = jnp.bfloat16, jnp.float32
    block, size = k_ref.shape
    groups = q_ref.shape[1] // size
    width = mixed_ref.shape[1]
    me = lax.axis_index("ctx")
    head = lax.axis_index("heads")
    outer, core = me // 2, me % 2
    outers = slots // 2
    twin = outer * 2 + 1 - core

    loads = []
    for c in range(heads):
        loads.append(
            pltpu.make_async_copy(
                weight_hbm.at[:, c * width : (c + 1) * width], projection.at[c], load_sem.at[c]
            )
        )
        loads[-1].start()

    barrier = pltpu.get_barrier_semaphore()
    line = [lax.rem(outer + o, outers) * 2 + core for o in range(1, outers)]
    for peer in [twin] + line:
        pl.semaphore_signal(barrier, inc=1, device_id={"ctx": peer}, device_id_type=MESH)
    for o in range(1, heads):
        pl.semaphore_signal(
            barrier, inc=1, device_id={"heads": lax.rem(head + o, heads)}, device_id_type=MESH
        )

    gate = gate_ref[...]
    high = gate.astype(bf16)
    middle = (gate - high.astype(f32)).astype(bf16)
    low = (gate - high.astype(f32) - middle.astype(f32)).astype(bf16)
    boundary = doc_ref[0]
    start = jnp.full((1, block), boundary, jnp.int32).astype(f32).astype(bf16)
    shared[me, :block, :] = k_ref[...]
    shared[me, block : 2 * block, :] = v_ref[...]
    shared[me, 2 * block :, :] = jnp.concatenate(
        [high.astype(f32), middle.astype(f32), low.astype(f32), start.astype(f32)]
        + [jnp.zeros((EXTRA - 4, block), f32)],
        axis=0,
    ).astype(bf16)

    pl.semaphore_wait(barrier, outers + heads - 1)

    def move(slot, peer, index):
        return pltpu.make_async_remote_copy(
            src_ref=shared.at[slot],
            dst_ref=shared.at[slot],
            send_sem=gather_send.at[index],
            recv_sem=gather_recv.at[slot],
            device_id={"ctx": peer},
            device_id_type=MESH,
        )

    sends = []
    for o, peer in enumerate(line):
        sends.append(move(me, peer, o))
        sends[-1].start()
    sends.append(move(me, twin, outers - 1))
    sends[-1].start()

    queries = jnp.concatenate([q_ref[:, g * size : (g + 1) * size] for g in range(groups)], axis=0)
    own = running_sum(jnp.broadcast_to(gate, (8, block)))[:1]
    cum_row = jnp.broadcast_to(own, (block, block))
    cum_col = cum_row.T
    at_t = lax.broadcasted_iota(jnp.int32, (block, block), 0)
    at_s = lax.broadcasted_iota(jnp.int32, (block, block), 1)
    allowed = (at_s <= at_t) & jnp.logical_not((at_s < boundary) & (at_t >= boundary))
    decay = jnp.where(allowed, jnp.exp(jnp.minimum(cum_col - cum_row, 0.0)), 0.0)
    read = jnp.where(at_t < boundary, jnp.exp(cum_col), 0.0)

    def part(keys, held, factor):
        products = lax.dot_general(queries, keys, NT, preferred_element_type=f32)
        scores = products * products * jnp.concatenate([factor] * groups, axis=0)
        return jnp.dot(scores.astype(bf16), held, preferred_element_type=f32)

    summed = part(k_ref[...], v_ref[...], decay)

    for o in range(1, outers):
        source = lax.rem(outer + outers - o, outers) * 2 + core
        move(source, twin, 0).wait_recv()
        sends.append(move(source, twin, outers - 1 + o))
        sends[-1].start()
    for o in range(outers):
        source = lax.rem(outer + outers - o, outers) * 2 + 1 - core
        move(source, twin, 0).wait_recv()

    tails = [shared[c, 2 * block :, :].astype(f32) for c in range(slots)]
    cumulative = running_sum(
        jnp.concatenate([tail[0:1] + tail[1:2] + tail[2:3] for tail in tails], axis=0)
    )
    token = lax.broadcasted_iota(jnp.int32, (1, block), 1)
    later = jnp.zeros((1, block), f32)
    alive = jnp.ones((1, block), f32)
    for c in range(slots - 1, -1, -1):
        before = (jnp.full((1, block), me, jnp.int32) > c).astype(f32)
        starts = tails[c][3:4].astype(jnp.int32)
        broken = starts < block
        begin = jnp.where(broken, starts, 0)
        row = cumulative[c : c + 1]
        total = jnp.broadcast_to(row[:, block - 1 : block], (1, block))
        weight = jnp.exp(total - row + later) * (alive * before)
        token_weight[:, c * block : (c + 1) * block] = jnp.where(token >= begin, weight, 0.0)
        later = later + total * before
        alive = alive * jnp.where(broken, 1.0 - before, 1.0)

    per = min(CHUNK, slots)
    for first in range(0, slots, per):
        keys = shared[first : first + per, :block, :].reshape(per * block, size)
        held = shared[first : first + per, block : 2 * block, :].reshape(per * block, size)
        factor = jnp.concatenate(
            [read * token_weight[:, (first + c) * block : (first + c + 1) * block] for c in range(per)],
            axis=1,
        )
        summed = summed + part(keys, held, factor)
    normed = summed * lax.rsqrt(jnp.mean(summed * summed, axis=-1, keepdims=True) + 1e-6)
    for g in range(groups):
        lanes = slice(g * size, (g + 1) * size)
        retained[:, lanes] = (normed[g * block : (g + 1) * block] * gain_ref[:, lanes]).astype(bf16)

    for load in loads:
        load.wait()
    parts = []
    for o in list(range(1, heads)) + [0]:
        target = lax.rem(head + o, heads)
        outgoing[o] = jnp.dot(
            retained[...], projection[target], preferred_element_type=f32
        ).astype(bf16)
        if o:
            parts.append(
                pltpu.make_async_remote_copy(
                    src_ref=outgoing.at[o],
                    dst_ref=incoming.at[o - 1],
                    send_sem=part_send.at[o - 1],
                    recv_sem=part_recv.at[o - 1],
                    device_id={"heads": target},
                    device_id_type=MESH,
                )
            )
            parts[-1].start()

    chunks = slots // per
    span = per * block

    def chunk(index):
        for c in range(per):
            lanes = slice(c * block, (c + 1) * block)
            turned = shared[index * per + c, :block, :].astype(f32).T
            keys_t[:, lanes] = turned.astype(bf16)
            weight = token_weight[:, pl.ds(pl.multiple_of((index * per + c) * block, block), block)]
            scaled[:, lanes] = turned * weight
            values[lanes, :] = shared[index * per + c, block : 2 * block, :]
        for a in range(size - 16, -1, -16):
            rows = size - a

            def step(s, carry):
                pieces = []
                firsts = []
                for u in range(PER_STEP):
                    i = a + 15 - (s * PER_STEP + u)
                    row = jnp.broadcast_to(scaled[pl.ds(i, 1), :], (16, span)).astype(jnp.bfloat16)
                    pieces.append(
                        (keys_t[a:, :].reshape(rows // 16, 16, span) * row[None]).reshape(rows, span)
                    )
                    firsts.append(i)
                product = jnp.dot(
                    jnp.concatenate(pieces, axis=0), values[...], preferred_element_type=jnp.float32
                )
                at = lax.broadcasted_iota(jnp.int32, (rows, size), 0) + a
                for u, i in enumerate(firsts):
                    piece = product[u * rows : (u + 1) * rows]
                    piece = jnp.where(at == i, piece, piece * ROOT_TWO)
                    place = pl.ds(offset(i, size) - (i - a), rows)
                    if chunks == 1:
                        acc[place, :] = piece
                    else:
                        acc[place, :] = acc[place, :] + jnp.where(at < i, 0.0, piece)
                return carry

            lax.fori_loop(0, 16 // PER_STEP, step, 0)

    if chunks == 1:
        chunk(0)
    else:
        acc[...] = jnp.zeros_like(acc)
        lax.fori_loop(0, chunks, lambda index, carry: (chunk(index), carry)[1], 0)
    prefix_ref[...] = acc[...].astype(bf16)

    for send in sends:
        send.wait_send()
    for send in parts:
        send.wait()
    total = outgoing[0].astype(f32)
    for o in range(1, heads):
        total = total + incoming[o - 1].astype(f32)
    mixed_ref[...] = total.astype(bf16)


def on_device(query_vectors, key_vectors, value_vectors, log_gate, doc_start, norm_gain, out_weight):
    bf16, f32 = jnp.bfloat16, jnp.float32
    block, _, size = key_vectors.shape
    row_width = query_vectors.shape[2]
    features = size * (size + 1) // 2
    slots = lax.axis_size("ctx")
    heads = lax.axis_size("heads")
    width = out_weight.shape[1] // heads
    span = min(CHUNK, slots) * block
    vmem = pl.BlockSpec(memory_space=pltpu.VMEM)
    mixed_out, prefix = pl.pallas_call(
        functools.partial(kernel, slots, heads),
        out_shape=(
            jax.ShapeDtypeStruct((block, width), bf16),
            jax.ShapeDtypeStruct((features, size), bf16),
        ),
        in_specs=[vmem] * 4
        + [pl.BlockSpec(memory_space=pltpu.SMEM), vmem, pl.BlockSpec(memory_space=pl.ANY)],
        out_specs=(vmem, vmem),
        scratch_shapes=[
            pltpu.VMEM((slots, 2 * block + EXTRA, size), bf16),
            pltpu.VMEM((1, slots * block), f32),
            pltpu.VMEM((heads, row_width, width), bf16),
            pltpu.VMEM((block, row_width), bf16),
            pltpu.VMEM((heads, block, width), bf16),
            pltpu.VMEM((heads - 1, block, width), bf16),
            pltpu.VMEM((size, span), bf16),
            pltpu.VMEM((size, span), f32),
            pltpu.VMEM((span, size), bf16),
            pltpu.VMEM((features, size), f32),
            pltpu.SemaphoreType.DMA((heads,)),
            pltpu.SemaphoreType.DMA((slots - 1,)),
            pltpu.SemaphoreType.DMA((slots,)),
            pltpu.SemaphoreType.DMA((heads - 1,)),
            pltpu.SemaphoreType.DMA((heads - 1,)),
        ],
        compiler_params=pltpu.CompilerParams(
            collective_id=0, has_side_effects=True, vmem_limit_bytes=56 * 2**20
        ),
    )(
        query_vectors[:, 0, :], key_vectors[:, 0, :], value_vectors[:, 0, :],
        log_gate, doc_start, norm_gain, out_weight,
    )
    return (mixed_out, prefix[None, None])


def solution(mesh):
    placed = (
        P("ctx", "heads", None),
        P("ctx", "heads", None),
        P("ctx", "heads", None),
        P("heads", "ctx"),
        P("ctx"),
        P("heads", None),
        P("heads", None),
    )
    return jax.shard_map(
        on_device,
        mesh=mesh,
        in_specs=placed,
        out_specs=(P("ctx", "heads"), P("heads", "ctx", None, None)),
        check_vma=False,
    )
```

```python
import functools
import math

import jax
import jax.numpy as jnp
from jax import lax
from jax.experimental import pallas as pl
from jax.experimental.pallas import tpu as pltpu
from jax.sharding import PartitionSpec as P

ROOT_TWO = math.sqrt(2.0)
NT = (((1,), (1,)), ((), ()))
MESH = pl.DeviceIdType.MESH
PER_STEP = 16
CHUNK = 8
EXTRA = 16


def offset(i, size):
    return i * size - i * (i - 1) // 2


def running_sum(rows):
    lane = lax.broadcasted_iota(jnp.int32, rows.shape, 1)
    shift = 1
    while shift < rows.shape[1]:
        rows = rows + jnp.where(lane >= shift, pltpu.roll(rows, shift, axis=1), 0.0)
        shift *= 2
    return rows


def kernel(
    slots, heads, q_ref, k_ref, v_ref, gate_ref, doc_ref, gain_ref, weight_hbm,
    mixed_ref, prefix_ref,
    shared, token_weight, projection, retained, outgoing, incoming, keys_t, scaled, values, acc,
    load_sem, gather_send, gather_recv, part_send, part_recv,
):
    bf16, f32 = jnp.bfloat16, jnp.float32
    block, size = k_ref.shape
    groups = q_ref.shape[1] // size
    width = mixed_ref.shape[1]
    me = lax.axis_index("ctx")
    head = lax.axis_index("heads")
    outer, core = me // 2, me % 2
    outers = slots // 2
    twin = outer * 2 + 1 - core

    loads = []
    for c in range(heads):
        loads.append(
            pltpu.make_async_copy(
                weight_hbm.at[:, c * width : (c + 1) * width], projection.at[c], load_sem.at[c]
            )
        )
        loads[-1].start()

    barrier = pltpu.get_barrier_semaphore()
    line = [lax.rem(outer + o, outers) * 2 + core for o in range(1, outers)]
    for peer in [twin] + line:
        pl.semaphore_signal(barrier, inc=1, device_id={"ctx": peer}, device_id_type=MESH)
    high_bit, low_bit = head // 2, head % 2
    first_peer = high_bit * 2 + 1 - low_bit
    second_peer = (1 - high_bit) * 2 + low_bit
    across = (1 - high_bit) * 2 + 1 - low_bit
    for peer in (first_peer, second_peer):
        pl.semaphore_signal(barrier, inc=1, device_id={"heads": peer}, device_id_type=MESH)

    gate = gate_ref[...]
    high = gate.astype(bf16)
    middle = (gate - high.astype(f32)).astype(bf16)
    low = (gate - high.astype(f32) - middle.astype(f32)).astype(bf16)
    boundary = doc_ref[0]
    start = jnp.full((1, block), boundary, jnp.int32).astype(f32).astype(bf16)
    shared[me, :block, :] = k_ref[...]
    shared[me, block : 2 * block, :] = v_ref[...]
    shared[me, 2 * block :, :] = jnp.concatenate(
        [high.astype(f32), middle.astype(f32), low.astype(f32), start.astype(f32)]
        + [jnp.zeros((EXTRA - 4, block), f32)],
        axis=0,
    ).astype(bf16)

    pl.semaphore_wait(barrier, outers + 2)

    def move(slot, peer, index):
        return pltpu.make_async_remote_copy(
            src_ref=shared.at[slot],
            dst_ref=shared.at[slot],
            send_sem=gather_send.at[index],
            recv_sem=gather_recv.at[slot],
            device_id={"ctx": peer},
            device_id_type=MESH,
        )

    sends = []
    for o, peer in enumerate(line):
        sends.append(move(me, peer, o))
        sends[-1].start()
    sends.append(move(me, twin, outers - 1))
    sends[-1].start()

    queries = jnp.concatenate([q_ref[:, g * size : (g + 1) * size] for g in range(groups)], axis=0)
    own = running_sum(jnp.broadcast_to(gate, (8, block)))[:1]
    cum_row = jnp.broadcast_to(own, (block, block))
    cum_col = cum_row.T
    at_t = lax.broadcasted_iota(jnp.int32, (block, block), 0)
    at_s = lax.broadcasted_iota(jnp.int32, (block, block), 1)
    allowed = (at_s <= at_t) & jnp.logical_not((at_s < boundary) & (at_t >= boundary))
    decay = jnp.where(allowed, jnp.exp(jnp.minimum(cum_col - cum_row, 0.0)), 0.0)
    read = jnp.where(at_t < boundary, jnp.exp(cum_col), 0.0)

    def part(keys, held, factor):
        products = lax.dot_general(queries, keys, NT, preferred_element_type=f32)
        scores = products * products * jnp.concatenate([factor] * groups, axis=0)
        return jnp.dot(scores.astype(bf16), held, preferred_element_type=f32)

    summed = part(k_ref[...], v_ref[...], decay)

    per = min(CHUNK, slots)
    chunks = slots // per
    span = per * block

    def turn(slot, index):
        lanes = pl.ds(pl.multiple_of(index * block, block), block)
        turned = shared[slot, :block, :].astype(f32).T
        keys_t[:, lanes] = turned.astype(bf16)
        scaled[:, lanes] = turned
        values[lanes, :] = shared[slot, block : 2 * block, :]

    if chunks == 1:
        turn(me, me)

    for o in range(1, outers):
        source = lax.rem(outer + outers - o, outers) * 2 + core
        move(source, twin, 0).wait_recv()
        sends.append(move(source, twin, outers - 1 + o))
        sends[-1].start()
        if chunks == 1:
            turn(source, source)
    for o in range(outers):
        source = lax.rem(outer + outers - o, outers) * 2 + 1 - core
        move(source, twin, 0).wait_recv()
        if chunks == 1:
            turn(source, source)

    tails = [shared[c, 2 * block :, :].astype(f32) for c in range(slots)]
    cumulative = running_sum(
        jnp.concatenate([tail[0:1] + tail[1:2] + tail[2:3] for tail in tails], axis=0)
    )
    token = lax.broadcasted_iota(jnp.int32, (1, block), 1)
    later = jnp.zeros((1, block), f32)
    alive = jnp.ones((1, block), f32)
    for c in range(slots - 1, -1, -1):
        before = (jnp.full((1, block), me, jnp.int32) > c).astype(f32)
        starts = tails[c][3:4].astype(jnp.int32)
        broken = starts < block
        begin = jnp.where(broken, starts, 0)
        row = cumulative[c : c + 1]
        total = jnp.broadcast_to(row[:, block - 1 : block], (1, block))
        weight = jnp.exp(total - row + later) * (alive * before)
        token_weight[:, c * block : (c + 1) * block] = jnp.where(token >= begin, weight, 0.0)
        later = later + total * before
        alive = alive * jnp.where(broken, 1.0 - before, 1.0)

    for first in range(0, slots, per):
        keys = shared[first : first + per, :block, :].reshape(per * block, size)
        held = shared[first : first + per, block : 2 * block, :].reshape(per * block, size)
        factor = jnp.concatenate(
            [read * token_weight[:, (first + c) * block : (first + c + 1) * block] for c in range(per)],
            axis=1,
        )
        summed = summed + part(keys, held, factor)
    normed = summed * lax.rsqrt(jnp.mean(summed * summed, axis=-1, keepdims=True) + 1e-6)
    for g in range(groups):
        lanes = slice(g * size, (g + 1) * size)
        retained[:, lanes] = (normed[g * block : (g + 1) * block] * gain_ref[:, lanes]).astype(bf16)

    half = width // 2

    def project(target, index):
        product = jnp.dot(retained[...], projection[target], preferred_element_type=f32).astype(bf16)
        outgoing[2 * index] = product[:, :half]
        outgoing[2 * index + 1] = product[:, half:]

    def part_copy(index, held, peer):
        return pltpu.make_async_remote_copy(
            src_ref=outgoing.at[held],
            dst_ref=incoming.at[index],
            send_sem=part_send.at[index],
            recv_sem=part_recv.at[index],
            device_id={"heads": peer},
            device_id_type=MESH,
        )

    copies = [
        part_copy(0, 6, first_peer),
        part_copy(1, 7, second_peer),
        part_copy(2, 2, first_peer),
        part_copy(3, 5, second_peer),
        part_copy(4, 3, first_peer),
        part_copy(5, 4, second_peer),
    ]
    for load in loads:
        load.wait()
    project(across, 3)
    copies[0].start()
    copies[1].start()
    project(first_peer, 1)
    copies[2].start()
    project(second_peer, 2)
    copies[3].start()
    project(head, 0)

    def pass_on():
        copies[1].wait_recv()
        outgoing[3] = (outgoing[3].astype(f32) + incoming[1].astype(f32)).astype(bf16)
        copies[4].start()
        copies[0].wait_recv()
        outgoing[4] = (outgoing[4].astype(f32) + incoming[0].astype(f32)).astype(bf16)
        copies[5].start()

    def chunk(index):
        if chunks == 1:
            scaled[...] = scaled[...] * token_weight[...]
        else:
            for c in range(per):
                lanes = slice(c * block, (c + 1) * block)
                turn(index * per + c, c)
                weight = token_weight[:, pl.ds(pl.multiple_of((index * per + c) * block, block), block)]
                scaled[:, lanes] = scaled[:, lanes] * weight
        for a in range(size - 16, -1, -16):
            rows = size - a

            def step(s, carry):
                pieces = []
                firsts = []
                for u in range(PER_STEP):
                    i = a + 15 - (s * PER_STEP + u)
                    row = jnp.broadcast_to(scaled[pl.ds(i, 1), :], (16, span)).astype(jnp.bfloat16)
                    pieces.append(
                        (keys_t[a:, :].reshape(rows // 16, 16, span) * row[None]).reshape(rows, span)
                    )
                    firsts.append(i)
                product = jnp.dot(
                    jnp.concatenate(pieces, axis=0), values[...], preferred_element_type=jnp.float32
                )
                at = lax.broadcasted_iota(jnp.int32, (rows, size), 0) + a
                for u, i in enumerate(firsts):
                    piece = product[u * rows : (u + 1) * rows]
                    piece = jnp.where(at == i, piece, piece * ROOT_TWO)
                    place = pl.ds(offset(i, size) - (i - a), rows)
                    if chunks == 1:
                        acc[place, :] = piece
                    else:
                        acc[place, :] = acc[place, :] + jnp.where(at < i, 0.0, piece)
                return carry

            lax.fori_loop(0, 16 // PER_STEP, step, 0)
            if chunks == 1 and a == size // 2:
                pass_on()

    if chunks == 1:
        chunk(0)
    else:
        pass_on()
        acc[...] = jnp.zeros_like(acc)
        lax.fori_loop(0, chunks, lambda index, carry: (chunk(index), carry)[1], 0)
    prefix_ref[...] = acc[...].astype(bf16)

    for send in sends:
        send.wait_send()
    for copy in copies:
        copy.wait_send()
    for copy in copies[2:]:
        copy.wait_recv()
    for side, (one, two) in enumerate(((2, 5), (3, 4))):
        total = outgoing[side].astype(f32) + incoming[one].astype(f32) + incoming[two].astype(f32)
        mixed_ref[:, side * half : (side + 1) * half] = total.astype(bf16)


def place_kernel(cuts, mixed_in, prefix_in, mixed_ref, prefix_ref, sems):
    rows = prefix_ref.shape[0] // cuts
    copies = [pltpu.make_async_copy(mixed_in, mixed_ref, sems.at[cuts])]
    for c in range(cuts):
        part = pl.ds(c * rows, rows)
        copies.append(pltpu.make_async_copy(prefix_in.at[part], prefix_ref.at[part], sems.at[c]))
    for copy in copies:
        copy.start()
    for copy in copies:
        copy.wait()


def on_device(query_vectors, key_vectors, value_vectors, log_gate, doc_start, norm_gain, out_weight):
    bf16, f32 = jnp.bfloat16, jnp.float32
    block, _, size = key_vectors.shape
    row_width = query_vectors.shape[2]
    features = size * (size + 1) // 2
    slots = lax.axis_size("ctx")
    heads = lax.axis_size("heads")
    width = out_weight.shape[1] // heads
    span = min(CHUNK, slots) * block
    vmem = pl.BlockSpec(memory_space=pltpu.VMEM)
    shapes = (
        jax.ShapeDtypeStruct((block, width), bf16),
        jax.ShapeDtypeStruct((features, size), bf16),
    )
    results = pl.pallas_call(
        functools.partial(kernel, slots, heads),
        out_shape=shapes,
        in_specs=[vmem] * 4
        + [pl.BlockSpec(memory_space=pltpu.SMEM), vmem, pl.BlockSpec(memory_space=pltpu.HBM)],
        out_specs=(vmem, vmem),
        scratch_shapes=[
            pltpu.VMEM((slots, 2 * block + EXTRA, size), bf16),
            pltpu.VMEM((1, slots * block), f32),
            pltpu.VMEM((heads, row_width, width), bf16),
            pltpu.VMEM((block, row_width), bf16),
            pltpu.VMEM((2 * heads, block, width // 2), bf16),
            pltpu.VMEM((6, block, width // 2), bf16),
            pltpu.VMEM((size, span), bf16),
            pltpu.VMEM((size, span), f32),
            pltpu.VMEM((span, size), bf16),
            pltpu.VMEM((features, size), f32),
            pltpu.SemaphoreType.DMA((heads,)),
            pltpu.SemaphoreType.DMA((slots - 1,)),
            pltpu.SemaphoreType.DMA((slots,)),
            pltpu.SemaphoreType.DMA((6,)),
            pltpu.SemaphoreType.DMA((6,)),
        ],
        compiler_params=pltpu.CompilerParams(
            collective_id=0, has_side_effects=True, vmem_limit_bytes=50 * 2**20
        ),
    )(
        query_vectors[:, 0, :], key_vectors[:, 0, :], value_vectors[:, 0, :],
        log_gate, doc_start, norm_gain, out_weight,
    )
    anywhere = pl.BlockSpec(memory_space=pl.ANY)
    cuts = 4 if features % 64 == 0 else 1
    mixed_out, prefix = pl.pallas_call(
        functools.partial(place_kernel, cuts),
        out_shape=shapes,
        in_specs=[anywhere] * 2,
        out_specs=(anywhere, anywhere),
        scratch_shapes=[pltpu.SemaphoreType.DMA((cuts + 1,))],
        compiler_params=pltpu.CompilerParams(vmem_limit_bytes=2**20),
    )(*results)
    return (mixed_out, prefix[None, None])


def solution(mesh):
    placed = (
        P("ctx", "heads", None),
        P("ctx", "heads", None),
        P("ctx", "heads", None),
        P("heads", "ctx"),
        P("ctx"),
        P("heads", None),
        P("heads", None),
    )
    return jax.shard_map(
        on_device,
        mesh=mesh,
        in_specs=placed,
        out_specs=(P("ctx", "heads"), P("heads", "ctx", None, None)),
        check_vma=False,
    )
```

```python
import functools
import math

import jax
import jax.numpy as jnp
from jax import lax
from jax.experimental import pallas as pl
from jax.experimental.pallas import tpu as pltpu
from jax.sharding import PartitionSpec as P

ROOT_TWO = math.sqrt(2.0)
NT = (((1,), (1,)), ((), ()))
MESH = pl.DeviceIdType.MESH
PER_STEP = 16
CHUNK = 8
EXTRA = 16


def offset(i, size):
    return i * size - i * (i - 1) // 2


def running_sum(rows):
    lane = lax.broadcasted_iota(jnp.int32, rows.shape, 1)
    shift = 1
    while shift < rows.shape[1]:
        rows = rows + jnp.where(lane >= shift, pltpu.roll(rows, shift, axis=1), 0.0)
        shift *= 2
    return rows


def kernel(
    slots, heads, q_ref, k_ref, v_ref, gate_ref, doc_ref, gain_ref, weight_hbm,
    mixed_ref, prefix_ref,
    shared, token_weight, projection, retained, outgoing, incoming, keys_t, scaled, values, acc, staged,
    store_sem, load_sem, gather_send, gather_recv, part_send, part_recv,
):
    bf16, f32 = jnp.bfloat16, jnp.float32
    block, size = k_ref.shape
    groups = q_ref.shape[1] // size
    width = mixed_ref.shape[1]
    me = lax.axis_index("ctx")
    head = lax.axis_index("heads")
    outer, core = me // 2, me % 2
    outers = slots // 2
    twin = outer * 2 + 1 - core

    loads = []
    for c in range(heads):
        loads.append(
            pltpu.make_async_copy(
                weight_hbm.at[:, c * width : (c + 1) * width], projection.at[c], load_sem.at[c]
            )
        )
        loads[-1].start()

    barrier = pltpu.get_barrier_semaphore()
    line = [lax.rem(outer + o, outers) * 2 + core for o in range(1, outers)]
    for peer in [twin] + line:
        pl.semaphore_signal(barrier, inc=1, device_id={"ctx": peer}, device_id_type=MESH)
    high_bit, low_bit = head // 2, head % 2
    first_peer = high_bit * 2 + 1 - low_bit
    second_peer = (1 - high_bit) * 2 + low_bit
    across = (1 - high_bit) * 2 + 1 - low_bit
    for peer in (first_peer, second_peer):
        pl.semaphore_signal(barrier, inc=1, device_id={"heads": peer}, device_id_type=MESH)

    gate = gate_ref[...]
    high = gate.astype(bf16)
    middle = (gate - high.astype(f32)).astype(bf16)
    low = (gate - high.astype(f32) - middle.astype(f32)).astype(bf16)
    boundary = doc_ref[0]
    start = jnp.full((1, block), boundary, jnp.int32).astype(f32).astype(bf16)
    shared[me, :block, :] = k_ref[...]
    shared[me, block : 2 * block, :] = v_ref[...]
    shared[me, 2 * block :, :] = jnp.concatenate(
        [high.astype(f32), middle.astype(f32), low.astype(f32), start.astype(f32)]
        + [jnp.zeros((EXTRA - 4, block), f32)],
        axis=0,
    ).astype(bf16)

    pl.semaphore_wait(barrier, outers + 2)

    def move(slot, peer, index):
        return pltpu.make_async_remote_copy(
            src_ref=shared.at[slot],
            dst_ref=shared.at[slot],
            send_sem=gather_send.at[index],
            recv_sem=gather_recv.at[slot],
            device_id={"ctx": peer},
            device_id_type=MESH,
        )

    sends = []
    for o, peer in enumerate(line):
        sends.append(move(me, peer, o))
        sends[-1].start()
    sends.append(move(me, twin, outers - 1))
    sends[-1].start()

    queries = jnp.concatenate([q_ref[:, g * size : (g + 1) * size] for g in range(groups)], axis=0)
    own = running_sum(jnp.broadcast_to(gate, (8, block)))[:1]
    cum_row = jnp.broadcast_to(own, (block, block))
    cum_col = cum_row.T
    at_t = lax.broadcasted_iota(jnp.int32, (block, block), 0)
    at_s = lax.broadcasted_iota(jnp.int32, (block, block), 1)
    allowed = (at_s <= at_t) & jnp.logical_not((at_s < boundary) & (at_t >= boundary))
    decay = jnp.where(allowed, jnp.exp(jnp.minimum(cum_col - cum_row, 0.0)), 0.0)
    read = jnp.where(at_t < boundary, jnp.exp(cum_col), 0.0)

    def part(keys, held, factor):
        products = lax.dot_general(queries, keys, NT, preferred_element_type=f32)
        scores = products * products * jnp.concatenate([factor] * groups, axis=0)
        return jnp.dot(scores.astype(bf16), held, preferred_element_type=f32)

    summed = part(k_ref[...], v_ref[...], decay)

    per = min(CHUNK, slots)
    chunks = slots // per
    span = per * block

    def turn(slot, index):
        lanes = pl.ds(pl.multiple_of(index * block, block), block)
        turned = shared[slot, :block, :].astype(f32).T
        keys_t[:, lanes] = turned.astype(bf16)
        scaled[:, lanes] = turned
        values[lanes, :] = shared[slot, block : 2 * block, :]

    if chunks == 1:
        turn(me, me)

    for o in range(1, outers):
        source = lax.rem(outer + outers - o, outers) * 2 + core
        move(source, twin, 0).wait_recv()
        sends.append(move(source, twin, outers - 1 + o))
        sends[-1].start()
        if chunks == 1:
            turn(source, source)
    for o in range(outers):
        source = lax.rem(outer + outers - o, outers) * 2 + 1 - core
        move(source, twin, 0).wait_recv()
        if chunks == 1:
            turn(source, source)

    tails = [shared[c, 2 * block :, :].astype(f32) for c in range(slots)]
    cumulative = running_sum(
        jnp.concatenate([tail[0:1] + tail[1:2] + tail[2:3] for tail in tails], axis=0)
    )
    token = lax.broadcasted_iota(jnp.int32, (1, block), 1)
    later = jnp.zeros((1, block), f32)
    alive = jnp.ones((1, block), f32)
    for c in range(slots - 1, -1, -1):
        before = (jnp.full((1, block), me, jnp.int32) > c).astype(f32)
        starts = tails[c][3:4].astype(jnp.int32)
        broken = starts < block
        begin = jnp.where(broken, starts, 0)
        row = cumulative[c : c + 1]
        total = jnp.broadcast_to(row[:, block - 1 : block], (1, block))
        weight = jnp.exp(total - row + later) * (alive * before)
        token_weight[:, c * block : (c + 1) * block] = jnp.where(token >= begin, weight, 0.0)
        later = later + total * before
        alive = alive * jnp.where(broken, 1.0 - before, 1.0)

    for first in range(0, slots, per):
        keys = shared[first : first + per, :block, :].reshape(per * block, size)
        held = shared[first : first + per, block : 2 * block, :].reshape(per * block, size)
        factor = jnp.concatenate(
            [read * token_weight[:, (first + c) * block : (first + c + 1) * block] for c in range(per)],
            axis=1,
        )
        summed = summed + part(keys, held, factor)
    normed = summed * lax.rsqrt(jnp.mean(summed * summed, axis=-1, keepdims=True) + 1e-6)
    for g in range(groups):
        lanes = slice(g * size, (g + 1) * size)
        retained[:, lanes] = (normed[g * block : (g + 1) * block] * gain_ref[:, lanes]).astype(bf16)

    half = width // 2

    def project(target, index):
        product = jnp.dot(retained[...], projection[target], preferred_element_type=f32).astype(bf16)
        outgoing[2 * index] = product[:, :half]
        outgoing[2 * index + 1] = product[:, half:]

    def part_copy(index, held, peer):
        return pltpu.make_async_remote_copy(
            src_ref=outgoing.at[held],
            dst_ref=incoming.at[index],
            send_sem=part_send.at[index],
            recv_sem=part_recv.at[index],
            device_id={"heads": peer},
            device_id_type=MESH,
        )

    copies = [
        part_copy(0, 6, first_peer),
        part_copy(1, 7, second_peer),
        part_copy(2, 2, first_peer),
        part_copy(3, 5, second_peer),
        part_copy(4, 3, first_peer),
        part_copy(5, 4, second_peer),
    ]
    for load in loads:
        load.wait()
    project(across, 3)
    copies[0].start()
    copies[1].start()
    project(first_peer, 1)
    copies[2].start()
    project(second_peer, 2)
    copies[3].start()
    project(head, 0)

    def pass_on():
        copies[1].wait_recv()
        outgoing[3] = (outgoing[3].astype(f32) + incoming[1].astype(f32)).astype(bf16)
        copies[4].start()
        copies[0].wait_recv()
        outgoing[4] = (outgoing[4].astype(f32) + incoming[0].astype(f32)).astype(bf16)
        copies[5].start()

    stores = []

    def emit(a):
        low_row = -(-offset(a, size) // 16) * 16
        high_row = prefix_ref.shape[0] if a == size - 16 else -(-offset(a + 16, size) // 16) * 16
        rows = pl.ds(low_row, high_row - low_row)
        staged[rows, :] = acc[rows, :].astype(bf16)
        stores.append(
            pltpu.make_async_copy(staged.at[rows], prefix_ref.at[rows], store_sem.at[a // 16])
        )
        stores[-1].start()

    def chunk(index):
        if chunks == 1:
            scaled[...] = scaled[...] * token_weight[...]
        else:
            for c in range(per):
                lanes = slice(c * block, (c + 1) * block)
                turn(index * per + c, c)
                weight = token_weight[:, pl.ds(pl.multiple_of((index * per + c) * block, block), block)]
                scaled[:, lanes] = scaled[:, lanes] * weight
        for a in range(size - 16, -1, -16):
            rows = size - a

            def step(s, carry):
                pieces = []
                firsts = []
                for u in range(PER_STEP):
                    i = a + 15 - (s * PER_STEP + u)
                    row = jnp.broadcast_to(scaled[pl.ds(i, 1), :], (16, span)).astype(jnp.bfloat16)
                    pieces.append(
                        (keys_t[a:, :].reshape(rows // 16, 16, span) * row[None]).reshape(rows, span)
                    )
                    firsts.append(i)
                product = jnp.dot(
                    jnp.concatenate(pieces, axis=0), values[...], preferred_element_type=jnp.float32
                )
                at = lax.broadcasted_iota(jnp.int32, (rows, size), 0) + a
                for u, i in enumerate(firsts):
                    piece = product[u * rows : (u + 1) * rows]
                    piece = jnp.where(at == i, piece, piece * ROOT_TWO)
                    place = pl.ds(offset(i, size) - (i - a), rows)
                    if chunks == 1:
                        acc[place, :] = piece
                    else:
                        acc[place, :] = acc[place, :] + jnp.where(at < i, 0.0, piece)
                return carry

            lax.fori_loop(0, 16 // PER_STEP, step, 0)
            if chunks == 1:
                emit(a)
            if chunks == 1 and a == size // 2:
                pass_on()

    if chunks == 1:
        chunk(0)
    else:
        pass_on()
        acc[...] = jnp.zeros_like(acc)
        lax.fori_loop(0, chunks, lambda index, carry: (chunk(index), carry)[1], 0)
        for a in range(size - 16, -1, -16):
            emit(a)

    for send in sends:
        send.wait_send()
    for copy in stores:
        copy.wait()
    for copy in copies:
        copy.wait_send()
    for copy in copies[2:]:
        copy.wait_recv()
    for side, (one, two) in enumerate(((2, 5), (3, 4))):
        total = outgoing[side].astype(f32) + incoming[one].astype(f32) + incoming[two].astype(f32)
        mixed_ref[:, side * half : (side + 1) * half] = total.astype(bf16)


def place_kernel(cuts, mixed_in, prefix_in, mixed_ref, prefix_ref, sems):
    rows = prefix_ref.shape[0] // cuts
    copies = [pltpu.make_async_copy(mixed_in, mixed_ref, sems.at[cuts])]
    for c in range(cuts):
        part = pl.ds(c * rows, rows)
        copies.append(pltpu.make_async_copy(prefix_in.at[part], prefix_ref.at[part], sems.at[c]))
    for copy in copies:
        copy.start()
    for copy in copies:
        copy.wait()


def on_device(query_vectors, key_vectors, value_vectors, log_gate, doc_start, norm_gain, out_weight):
    bf16, f32 = jnp.bfloat16, jnp.float32
    block, _, size = key_vectors.shape
    row_width = query_vectors.shape[2]
    features = size * (size + 1) // 2
    slots = lax.axis_size("ctx")
    heads = lax.axis_size("heads")
    width = out_weight.shape[1] // heads
    span = min(CHUNK, slots) * block
    vmem = pl.BlockSpec(memory_space=pltpu.VMEM)
    shapes = (
        jax.ShapeDtypeStruct((block, width), bf16),
        jax.ShapeDtypeStruct((features, size), bf16),
    )
    results = pl.pallas_call(
        functools.partial(kernel, slots, heads),
        out_shape=shapes,
        in_specs=[vmem] * 4
        + [pl.BlockSpec(memory_space=pltpu.SMEM), vmem, pl.BlockSpec(memory_space=pltpu.HBM)],
        out_specs=(vmem, pl.BlockSpec(memory_space=pl.ANY)),
        scratch_shapes=[
            pltpu.VMEM((slots, 2 * block + EXTRA, size), bf16),
            pltpu.VMEM((1, slots * block), f32),
            pltpu.VMEM((heads, row_width, width), bf16),
            pltpu.VMEM((block, row_width), bf16),
            pltpu.VMEM((2 * heads, block, width // 2), bf16),
            pltpu.VMEM((6, block, width // 2), bf16),
            pltpu.VMEM((size, span), bf16),
            pltpu.VMEM((size, span), f32),
            pltpu.VMEM((span, size), bf16),
            pltpu.VMEM((features, size), f32),
            pltpu.VMEM((features, size), bf16),
            pltpu.SemaphoreType.DMA((size // 16,)),
            pltpu.SemaphoreType.DMA((heads,)),
            pltpu.SemaphoreType.DMA((slots - 1,)),
            pltpu.SemaphoreType.DMA((slots,)),
            pltpu.SemaphoreType.DMA((6,)),
            pltpu.SemaphoreType.DMA((6,)),
        ],
        compiler_params=pltpu.CompilerParams(
            collective_id=0, has_side_effects=True, vmem_limit_bytes=54 * 2**20
        ),
    )(
        query_vectors[:, 0, :], key_vectors[:, 0, :], value_vectors[:, 0, :],
        log_gate, doc_start, norm_gain, out_weight,
    )
    anywhere = pl.BlockSpec(memory_space=pl.ANY)
    cuts = 4 if features % 64 == 0 else 1
    mixed_out, prefix = pl.pallas_call(
        functools.partial(place_kernel, cuts),
        out_shape=shapes,
        in_specs=[anywhere] * 2,
        out_specs=(anywhere, anywhere),
        scratch_shapes=[pltpu.SemaphoreType.DMA((cuts + 1,))],
        compiler_params=pltpu.CompilerParams(vmem_limit_bytes=54 * 2**20),
    )(*results)
    return (mixed_out, prefix[None, None])


def solution(mesh):
    placed = (
        P("ctx", "heads", None),
        P("ctx", "heads", None),
        P("ctx", "heads", None),
        P("heads", "ctx"),
        P("ctx"),
        P("heads", None),
        P("heads", None),
    )
    return jax.shard_map(
        on_device,
        mesh=mesh,
        in_specs=placed,
        out_specs=(P("ctx", "heads"), P("heads", "ctx", None, None)),
        check_vma=False,
    )
```

```python
import functools
import math

import jax
import jax.numpy as jnp
from jax import lax
from jax.experimental import pallas as pl
from jax.experimental.pallas import tpu as pltpu
from jax.sharding import PartitionSpec as P

ROOT_TWO = math.sqrt(2.0)
NT = (((1,), (1,)), ((), ()))
MESH = pl.DeviceIdType.MESH
PER_STEP = 16
CHUNK = 8
EXTRA = 16


def offset(i, size):
    return i * size - i * (i - 1) // 2


def running_sum(rows):
    lane = lax.broadcasted_iota(jnp.int32, rows.shape, 1)
    shift = 1
    while shift < rows.shape[1]:
        rows = rows + jnp.where(lane >= shift, pltpu.roll(rows, shift, axis=1), 0.0)
        shift *= 2
    return rows


def kernel(
    slots, heads, q_ref, k_ref, v_ref, gate_ref, doc_ref, gain_ref, weight_hbm,
    mixed_ref, prefix_ref,
    shared, token_weight, projection, retained, outgoing, incoming, keys_t, scaled, values, acc, staged,
    store_sem, load_sem, gather_send, gather_recv, part_send, part_recv,
):
    bf16, f32 = jnp.bfloat16, jnp.float32
    block, size = k_ref.shape
    groups = q_ref.shape[1] // size
    width = mixed_ref.shape[1]
    me = lax.axis_index("ctx")
    head = lax.axis_index("heads")
    outer, core = me // 2, me % 2
    outers = slots // 2
    twin = outer * 2 + 1 - core

    loads = []
    for c in range(heads):
        loads.append(
            pltpu.make_async_copy(
                weight_hbm.at[:, c * width : (c + 1) * width], projection.at[c], load_sem.at[c]
            )
        )
        loads[-1].start()

    barrier = pltpu.get_barrier_semaphore()
    line = [lax.rem(outer + o, outers) * 2 + core for o in range(1, outers)]
    for peer in [twin] + line:
        pl.semaphore_signal(barrier, inc=1, device_id={"ctx": peer}, device_id_type=MESH)
    high_bit, low_bit = head // 2, head % 2
    first_peer = high_bit * 2 + 1 - low_bit
    second_peer = (1 - high_bit) * 2 + low_bit
    across = (1 - high_bit) * 2 + 1 - low_bit
    for peer in (first_peer, second_peer):
        pl.semaphore_signal(barrier, inc=1, device_id={"heads": peer}, device_id_type=MESH)

    gate = gate_ref[...]
    high = gate.astype(bf16)
    middle = (gate - high.astype(f32)).astype(bf16)
    low = (gate - high.astype(f32) - middle.astype(f32)).astype(bf16)
    boundary = doc_ref[0]
    start = jnp.full((1, block), boundary, jnp.int32).astype(f32).astype(bf16)
    shared[me, :block, :] = k_ref[...]
    shared[me, block : 2 * block, :] = v_ref[...]
    shared[me, 2 * block :, :] = jnp.concatenate(
        [high.astype(f32), middle.astype(f32), low.astype(f32), start.astype(f32)]
        + [jnp.zeros((EXTRA - 4, block), f32)],
        axis=0,
    ).astype(bf16)

    pl.semaphore_wait(barrier, outers + 2)

    def move(slot, peer, index):
        return pltpu.make_async_remote_copy(
            src_ref=shared.at[slot],
            dst_ref=shared.at[slot],
            send_sem=gather_send.at[index],
            recv_sem=gather_recv.at[slot],
            device_id={"ctx": peer},
            device_id_type=MESH,
        )

    sends = []
    for o, peer in enumerate(line):
        sends.append(move(me, peer, o))
        sends[-1].start()
    sends.append(move(me, twin, outers - 1))
    sends[-1].start()

    queries = jnp.concatenate([q_ref[:, g * size : (g + 1) * size] for g in range(groups)], axis=0)
    own = running_sum(jnp.broadcast_to(gate, (8, block)))[:1]
    cum_row = jnp.broadcast_to(own, (block, block))
    cum_col = cum_row.T
    at_t = lax.broadcasted_iota(jnp.int32, (block, block), 0)
    at_s = lax.broadcasted_iota(jnp.int32, (block, block), 1)
    allowed = (at_s <= at_t) & jnp.logical_not((at_s < boundary) & (at_t >= boundary))
    decay = jnp.where(allowed, jnp.exp(jnp.minimum(cum_col - cum_row, 0.0)), 0.0)
    read = jnp.where(at_t < boundary, jnp.exp(cum_col), 0.0)

    def part(keys, held, factor):
        products = lax.dot_general(queries, keys, NT, preferred_element_type=f32)
        scores = products * products * jnp.concatenate([factor] * groups, axis=0)
        return jnp.dot(scores.astype(bf16), held, preferred_element_type=f32)

    summed = part(k_ref[...], v_ref[...], decay)

    per = min(CHUNK, slots)
    chunks = slots // per
    span = per * block

    def turn(slot, index):
        lanes = pl.ds(pl.multiple_of(index * block, block), block)
        turned = shared[slot, :block, :].astype(f32).T
        keys_t[:, lanes] = turned.astype(bf16)
        scaled[:, lanes] = turned
        values[lanes, :] = shared[slot, block : 2 * block, :]

    if chunks == 1:
        turn(me, me)

    for o in range(1, outers):
        source = lax.rem(outer + outers - o, outers) * 2 + core
        move(source, twin, 0).wait_recv()
        sends.append(move(source, twin, outers - 1 + o))
        sends[-1].start()
        if chunks == 1:
            turn(source, source)
    for o in range(outers):
        source = lax.rem(outer + outers - o, outers) * 2 + 1 - core
        move(source, twin, 0).wait_recv()
        if chunks == 1:
            turn(source, source)

    tails = [shared[c, 2 * block :, :].astype(f32) for c in range(slots)]
    cumulative = running_sum(
        jnp.concatenate([tail[0:1] + tail[1:2] + tail[2:3] for tail in tails], axis=0)
    )
    token = lax.broadcasted_iota(jnp.int32, (1, block), 1)
    later = jnp.zeros((1, block), f32)
    alive = jnp.ones((1, block), f32)
    for c in range(slots - 1, -1, -1):
        before = (jnp.full((1, block), me, jnp.int32) > c).astype(f32)
        starts = tails[c][3:4].astype(jnp.int32)
        broken = starts < block
        begin = jnp.where(broken, starts, 0)
        row = cumulative[c : c + 1]
        total = jnp.broadcast_to(row[:, block - 1 : block], (1, block))
        weight = jnp.exp(total - row + later) * (alive * before)
        token_weight[:, c * block : (c + 1) * block] = jnp.where(token >= begin, weight, 0.0)
        later = later + total * before
        alive = alive * jnp.where(broken, 1.0 - before, 1.0)

    for first in range(0, slots, per):
        keys = shared[first : first + per, :block, :].reshape(per * block, size)
        held = shared[first : first + per, block : 2 * block, :].reshape(per * block, size)
        factor = jnp.concatenate(
            [read * token_weight[:, (first + c) * block : (first + c + 1) * block] for c in range(per)],
            axis=1,
        )
        summed = summed + part(keys, held, factor)
    normed = summed * lax.rsqrt(jnp.mean(summed * summed, axis=-1, keepdims=True) + 1e-6)
    for g in range(groups):
        lanes = slice(g * size, (g + 1) * size)
        retained[:, lanes] = (normed[g * block : (g + 1) * block] * gain_ref[:, lanes]).astype(bf16)

    half = width // 2

    def project(target, index):
        product = jnp.dot(retained[...], projection[target], preferred_element_type=f32).astype(bf16)
        outgoing[2 * index] = product[:, :half]
        outgoing[2 * index + 1] = product[:, half:]

    def part_copy(index, held, peer):
        return pltpu.make_async_remote_copy(
            src_ref=outgoing.at[held],
            dst_ref=incoming.at[index],
            send_sem=part_send.at[index],
            recv_sem=part_recv.at[index],
            device_id={"heads": peer},
            device_id_type=MESH,
        )

    copies = [
        part_copy(0, 6, first_peer),
        part_copy(1, 7, second_peer),
        part_copy(2, 2, first_peer),
        part_copy(3, 5, second_peer),
        part_copy(4, 3, first_peer),
        part_copy(5, 4, second_peer),
    ]
    for load in loads:
        load.wait()
    project(across, 3)
    copies[0].start()
    copies[1].start()
    project(first_peer, 1)
    copies[2].start()
    project(second_peer, 2)
    copies[3].start()
    project(head, 0)

    def pass_on():
        copies[1].wait_recv()
        outgoing[3] = (outgoing[3].astype(f32) + incoming[1].astype(f32)).astype(bf16)
        copies[4].start()
        copies[0].wait_recv()
        outgoing[4] = (outgoing[4].astype(f32) + incoming[0].astype(f32)).astype(bf16)
        copies[5].start()

    stores = []

    def emit(a):
        low_row = -(-offset(a, size) // 16) * 16
        high_row = prefix_ref.shape[0] if a == size - 16 else -(-offset(a + 16, size) // 16) * 16
        rows = pl.ds(low_row, high_row - low_row)
        staged[rows, :] = acc[rows, :].astype(bf16)
        stores.append(
            pltpu.make_async_copy(staged.at[rows], prefix_ref.at[rows], store_sem.at[a // 16])
        )
        stores[-1].start()

    def chunk(index):
        if chunks == 1:
            scaled[...] = scaled[...] * token_weight[...]
        else:
            for c in range(per):
                lanes = slice(c * block, (c + 1) * block)
                turn(index * per + c, c)
                weight = token_weight[:, pl.ds(pl.multiple_of((index * per + c) * block, block), block)]
                scaled[:, lanes] = scaled[:, lanes] * weight
        for a in range(size - 16, -1, -16):
            rows = size - a

            def step(s, carry):
                pieces = []
                firsts = []
                for u in range(PER_STEP):
                    i = a + 15 - (s * PER_STEP + u)
                    row = jnp.broadcast_to(scaled[pl.ds(i, 1), :], (16, span)).astype(jnp.bfloat16)
                    pieces.append(
                        (keys_t[a:, :].reshape(rows // 16, 16, span) * row[None]).reshape(rows, span)
                    )
                    firsts.append(i)
                product = jnp.dot(
                    jnp.concatenate(pieces, axis=0), values[...], preferred_element_type=jnp.float32
                )
                at = lax.broadcasted_iota(jnp.int32, (rows, size), 0) + a
                for u, i in enumerate(firsts):
                    piece = product[u * rows : (u + 1) * rows]
                    piece = jnp.where(at == i, piece, piece * ROOT_TWO)
                    place = pl.ds(offset(i, size) - (i - a), rows)
                    if chunks == 1:
                        acc[place, :] = piece
                    else:
                        acc[place, :] = acc[place, :] + jnp.where(at < i, 0.0, piece)
                return carry

            lax.fori_loop(0, 16 // PER_STEP, step, 0)
            if chunks == 1:
                emit(a)
            if chunks == 1 and a == size // 2:
                pass_on()

    if chunks == 1:
        chunk(0)
    else:
        pass_on()
        acc[...] = jnp.zeros_like(acc)
        lax.fori_loop(0, chunks, lambda index, carry: (chunk(index), carry)[1], 0)
        for a in range(size - 16, -1, -16):
            emit(a)

    for send in sends:
        send.wait_send()
    for copy in stores:
        copy.wait()
    for copy in copies:
        copy.wait_send()
    for copy in copies[2:]:
        copy.wait_recv()
    for side, (one, two) in enumerate(((2, 5), (3, 4))):
        total = outgoing[side].astype(f32) + incoming[one].astype(f32) + incoming[two].astype(f32)
        mixed_ref[:, side * half : (side + 1) * half] = total.astype(bf16)


def place_kernel(cuts, mixed_in, prefix_in, mixed_ref, prefix_ref, mixed_held, prefix_held, sems):
    rows = prefix_ref.shape[0] // cuts
    inward = []
    outward = []
    for c in range(cuts):
        part = pl.ds(c * rows, rows)
        inward.append(
            pltpu.make_async_copy(prefix_in.at[part], prefix_held.at[part], sems.at[0, c])
        )
        outward.append(
            pltpu.make_async_copy(prefix_held.at[part], prefix_ref.at[part], sems.at[1, c])
        )
    inward.append(pltpu.make_async_copy(mixed_in, mixed_held, sems.at[0, cuts]))
    outward.append(pltpu.make_async_copy(mixed_held, mixed_ref, sems.at[1, cuts]))
    for copy in inward:
        copy.start()
    for get, put in zip(inward, outward):
        get.wait()
        put.start()
    for copy in outward:
        copy.wait()


def on_device(query_vectors, key_vectors, value_vectors, log_gate, doc_start, norm_gain, out_weight):
    bf16, f32 = jnp.bfloat16, jnp.float32
    block, _, size = key_vectors.shape
    row_width = query_vectors.shape[2]
    features = size * (size + 1) // 2
    slots = lax.axis_size("ctx")
    heads = lax.axis_size("heads")
    width = out_weight.shape[1] // heads
    span = min(CHUNK, slots) * block
    vmem = pl.BlockSpec(memory_space=pltpu.VMEM)
    shapes = (
        jax.ShapeDtypeStruct((block, width), bf16),
        jax.ShapeDtypeStruct((features, size), bf16),
    )
    results = pl.pallas_call(
        functools.partial(kernel, slots, heads),
        out_shape=shapes,
        in_specs=[vmem] * 4
        + [pl.BlockSpec(memory_space=pltpu.SMEM), vmem, pl.BlockSpec(memory_space=pltpu.HBM)],
        out_specs=(vmem, pl.BlockSpec(memory_space=pl.ANY)),
        scratch_shapes=[
            pltpu.VMEM((slots, 2 * block + EXTRA, size), bf16),
            pltpu.VMEM((1, slots * block), f32),
            pltpu.VMEM((heads, row_width, width), bf16),
            pltpu.VMEM((block, row_width), bf16),
            pltpu.VMEM((2 * heads, block, width // 2), bf16),
            pltpu.VMEM((6, block, width // 2), bf16),
            pltpu.VMEM((size, span), bf16),
            pltpu.VMEM((size, span), f32),
            pltpu.VMEM((span, size), bf16),
            pltpu.VMEM((features, size), f32),
            pltpu.VMEM((features, size), bf16),
            pltpu.SemaphoreType.DMA((size // 16,)),
            pltpu.SemaphoreType.DMA((heads,)),
            pltpu.SemaphoreType.DMA((slots - 1,)),
            pltpu.SemaphoreType.DMA((slots,)),
            pltpu.SemaphoreType.DMA((6,)),
            pltpu.SemaphoreType.DMA((6,)),
        ],
        compiler_params=pltpu.CompilerParams(
            collective_id=0, has_side_effects=True, vmem_limit_bytes=54 * 2**20
        ),
    )(
        query_vectors[:, 0, :], key_vectors[:, 0, :], value_vectors[:, 0, :],
        log_gate, doc_start, norm_gain, out_weight,
    )
    anywhere = pl.BlockSpec(memory_space=pl.ANY)
    cuts = 4 if features % 64 == 0 else 1
    mixed_out, prefix = pl.pallas_call(
        functools.partial(place_kernel, cuts),
        out_shape=shapes,
        in_specs=[anywhere] * 2,
        out_specs=(anywhere, anywhere),
        scratch_shapes=[
            pltpu.VMEM((block, width), bf16),
            pltpu.VMEM((features, size), bf16),
            pltpu.SemaphoreType.DMA((2, cuts + 1)),
        ],
        compiler_params=pltpu.CompilerParams(vmem_limit_bytes=54 * 2**20),
    )(*results)
    return (mixed_out, prefix[None, None])


def solution(mesh):
    placed = (
        P("ctx", "heads", None),
        P("ctx", "heads", None),
        P("ctx", "heads", None),
        P("heads", "ctx"),
        P("ctx"),
        P("heads", None),
        P("heads", None),
    )
    return jax.shard_map(
        on_device,
        mesh=mesh,
        in_specs=placed,
        out_specs=(P("ctx", "heads"), P("heads", "ctx", None, None)),
        check_vma=False,
    )
```
